512 devices in a mesh: row: 64 (over y_lo, z, core), col: 8 (over y_hi, x).
Axes of the slice: x: 4, y: 8 (y_hi: 2, y_lo: 4; y = y_hi * 4 + y_lo), z: 8, core: 2. Of those that a mesh axis runs over, the one named last changes fastest.
Arguments:
- vectors: float32 [32768, 1024], P('row', 'col'), may hold values from -6 to 6
- householder: float32 [2, 32768, 256], P(None, 'row', 'col'), may hold values from -0.03125 to 0.03125
- tfactors: float32 [2, 256, 256], P(None, None, 'col'), may hold values from -0.17 to 2, as said below
Outputs:
- transformed: float32 [32768, 1024], P('row', 'col')
The draws below stay inside these ranges and needn't reach their ends.
Inputs may be any that keep to these rules, and one draw needn't show every extreme that they name: Each tfactors[b] is upper triangular with a positive diagonal between 1 and 2.
All inputs are finite; a program needn't handle non-finite values.
Results may differ from the reference program's by a relative error of at most 0.0001.
Values sent between devices are 32-bit elements; how exact they have to be, the bound alone decides.
A program may use at most 64 MiB of HBM per device.

```python
import jax
import jax.numpy as jnp
from jax import lax

N = 32768
NB = 256
BLOCKS = 2
M = 1024


def draw_tfactors(key, part):
    key_off, key_diag = jax.random.split(jax.random.fold_in(key, 17))
    offdiag = jax.random.uniform(key_off, (BLOCKS, NB, NB), jnp.float32, -0.17, 0.17)
    diagonal = jnp.exp(jax.random.uniform(key_diag, (BLOCKS, NB), jnp.float32, 0.0, 0.69))
    upper = jnp.triu(offdiag, 1)
    identity = jnp.eye(NB, dtype=jnp.float32)
    return upper + diagonal[:, :, None] * identity[None, :, :]


def block_levels(rng, dims, shards, smallest, largest):
    def one(dim, shards_of):
        draws = jax.random.uniform(jax.random.fold_in(jax.random.fold_in(rng, 6), dim), (shards_of,), jnp.float32, smallest / len(shards), largest / len(shards))
        return jnp.repeat(jnp.exp(draws), dims[dim] // shards_of).reshape((-1,) + (1,) * (len(dims) - dim - 1))

    gain = one(*shards[0])
    for cut in shards[1:]:
        gain = gain * one(*cut)
    return gain


def noise(own_key, shape, deviation, most, pieces=(), held_as=jnp.bfloat16):
    level = block_levels(own_key, shape, pieces, -0.22, 0.18) if pieces else 1.0
    values = jax.random.normal(own_key, shape, jnp.float32) * deviation * level
    return jnp.minimum(jnp.maximum(values, -most), most).astype(held_as)


def setup_inputs(seed: int = 0) -> dict:
    seeds = jax.random.split(jax.random.key(seed), 4)
    return {
        "vectors": noise(seeds[0], (N, M), 1.0, 6.0, ((0, 64), (1, 8)), jnp.float32),
        "householder": noise(seeds[1], (BLOCKS, N, NB), N ** -0.5, 0.03125, ((1, 64), (2, 8)), jnp.float32),
        "tfactors": draw_tfactors(jax.random.fold_in(seeds[3], 71), 0),
    }


def project(current, blockv):
    return lax.dot_general(current, blockv, (((0,), (0,)), ((), ())), precision=lax.Precision.HIGHEST, preferred_element_type=jnp.float32)


def reference(vectors, householder, tfactors):
    current = vectors
    for block in range(BLOCKS):
        blockv = householder[block]
        blockt = tfactors[block]
        products_t = project(current, blockv)
        reflect_t = lax.dot_general(products_t, blockt, (((1,), (1,)), ((), ())), precision=lax.Precision.HIGHEST, preferred_element_type=jnp.float32)
        current = current - lax.dot_general(blockv, reflect_t, (((1,), (1,)), ((), ())), precision=lax.Precision.HIGHEST, preferred_element_type=jnp.float32)
    return current
```

```python
import functools

import jax
import jax.numpy as jnp
from jax import lax
from jax.experimental import pallas as pl
from jax.experimental.pallas import tpu as pltpu
from jax.sharding import PartitionSpec as P

MESH = pl.DeviceIdType.MESH
F32 = jnp.float32
BF16 = jnp.bfloat16
YL, NZ, CORES = 4, 8, 2
YH, NX = 2, 4
NT = (((1,), (1,)), ((), ()))
NN = (((1,), (0,)), ((), ()))


def split(value):
    high = value.astype(BF16)
    return high, (value - high.astype(F32)).astype(BF16)


def dot3(a, b, dims):
    def one(left, right):
        return lax.dot_general(left, right, dims, preferred_element_type=F32)

    return one(a[0], b[0]) + (one(a[0], b[1]) + one(a[1], b[0]))


class Copies:
    def __init__(self, send, recv):
        self.send, self.recv, self.used, self.open = send, recv, 0, []

    def start(self, src, dst, device):
        at = self.used
        self.used += 1
        copy = pltpu.make_async_remote_copy(
            src_ref=src,
            dst_ref=dst,
            send_sem=self.send.at[at],
            recv_sem=self.recv.at[at],
            device_id=device,
            device_id_type=MESH,
        )
        copy.start()
        self.open.append(copy)
        return copy

    def finish(self):
        for copy in self.open:
            copy.wait_send()


N_COPIES = 2 * 7 + 7 + 2 * (1 + 3 + 7 + 3 + 4) + 31 + 1


def kernel(
    v_in, t_in, c_in, out_ref,
    vt, tt, c_v, lhs_h, lhs_l,
    pp0, pp1, cr0, cr1, s10, s11, yr0, yr1, s20, s21, zr0, zr1, pf0, pf1, gf,
    w1h, w1l, v0h, v0l,
    local_sem, send_sem, recv_sem,
):
    row, col = lax.axis_index("row"), lax.axis_index("col")
    core, z, yl = lax.rem(row, 2), lax.rem(row // 2, NZ), row // (2 * NZ)
    x, yh = lax.rem(col, NX), col // NX

    def at(dc=0, dz=0, dyl=0, dx=0, dyh=0):
        r = (lax.rem(yl + dyl, YL) * NZ + lax.rem(z + dz, NZ)) * 2 + lax.rem(core + dc, 2)
        c = lax.rem(yh + dyh, YH) * NX + lax.rem(x + dx, NX)
        return (r, c)

    other_col = lax.rem(yh + 1, YH) * NX + x
    loads = [
        pltpu.make_async_copy(v_in.at[0], vt.at[0, col], local_sem.at[0]),
        pltpu.make_async_copy(v_in.at[1], vt.at[1, col], local_sem.at[1]),
        pltpu.make_async_copy(c_in, c_v, local_sem.at[2]),
        pltpu.make_async_copy(t_in, tt.at[col], local_sem.at[3]),
    ]
    for load in loads:
        load.start()

    barrier = pltpu.get_barrier_semaphore()
    partners = [at(dyh=1)]
    partners += [at(dz=d) for d in (4, 3, 5, 2, 6, 1, 7)]
    partners += [at(dyl=d) for d in (1, 2, 3)] + [at(dx=d) for d in (2, 1, 3)] + [at(dc=1)]
    for device in partners:
        pl.semaphore_signal(barrier, inc=1, device_id=device, device_id_type=MESH)
    loads[0].wait()
    loads[1].wait()
    pl.semaphore_wait(barrier, len(partners))

    copies = Copies(send_sem, recv_sem)

    def along_x(ref):
        return [copies.start(ref, ref, at(dx=d)) for d in (2, 1, 3)]

    v_own, v_far, v_far_x = [None] * 2, [None] * 2, [None] * 2
    for b in range(2):
        mine = vt.at[b, col]
        v_far[b] = copies.start(mine, mine, at(dyh=1))
        v_own[b] = along_x(mine)
    loads[3].wait()
    t_far = copies.start(tt.at[col], tt.at[col], at(dyh=1))

    loads[2].wait()
    for part in range(2):
        turned = jnp.transpose(c_v[pl.ds(256 * part, 256), :])
        high, low = split(turned)
        lhs_h[0:128, 256 * part : 256 * (part + 1)] = high
        lhs_l[0:128, 256 * part : 256 * (part + 1)] = low
    high, low = split(vt[1, col])
    lhs_h[128:160, :] = high
    lhs_l[128:160, :] = low

    for b in range(2):
        v_far[b].wait_recv()
        v_far_x[b] = along_x(vt.at[b, other_col])
    t_own = along_x(tt.at[col])
    t_far.wait_recv()
    t_far_x = along_x(tt.at[other_col])

    def project(b, half):
        rows = 160 if b == 0 else 128
        blockv = split(vt[b, pl.ds(half * NX, NX)].reshape(128, 512))
        value = dot3((lhs_h[0:rows, :], lhs_l[0:rows, :]), blockv, NT)
        pp = (pp0, pp1)[b]
        for h in range(2):
            for s in range(YL):
                first = 64 * h + 16 * s
                pp[h, s, pl.ds(2 * half, 2)] = value[first : first + 16].reshape(2, 8, 128)
        if b == 0:
            for s in range(YL):
                pp[half, s, 4] = value[128 + 8 * s : 136 + 8 * s]

    for b in range(2):
        for copy in v_own[b]:
            copy.wait_recv()
        project(b, yh)

    pps, crs, s1s, yrs, s2s, zrs, pfs = (
        (pp0, pp1), (cr0, cr1), (s10, s11), (yr0, yr1), (s20, s21), (zr0, zr1), (pf0, pf1),
    )
    across = [None] * 2
    for b in range(2):
        for copy in v_far_x[b]:
            copy.wait_recv()
        project(b, lax.rem(yh + 1, YH))
        across[b] = copies.start(pps[b].at[1 - core], crs[b], at(dc=1))

    down = [None] * 2
    for b in range(2):
        across[b].wait_recv()
        s1s[b][...] = pps[b][core] + crs[b][...]
        down[b] = [
            copies.start(s1s[b].at[lax.rem(yl + d, YL)], yrs[b].at[d - 1], at(dyl=d))
            for d in (3, 2, 1)
        ]

    around = [None] * 2
    for b in range(2):
        for copy in down[b]:
            copy.wait_recv()
        s2s[b][...] = s1s[b][yl] + yrs[b][0] + yrs[b][1] + yrs[b][2]
        around[b] = [
            copies.start(s2s[b], zrs[b].at[d - 1], at(dz=d)) for d in (4, 3, 5, 2, 6, 1, 7)
        ]

    for copy in t_own + t_far_x:
        copy.wait_recv()
    high, low = split(jnp.transpose(vt[0].reshape(256, 512)))
    v0h[...] = high
    v0l[...] = low
    t1 = split(tt[:, 1].reshape(256, 256))
    high, low = split(dot3(split(jnp.transpose(vt[1].reshape(256, 512))), t1, NT))
    w1h[...] = high
    w1l[...] = low

    up, over, g_out = [None] * 2, [None] * 2, []
    for b in range(2):
        for copy in around[b]:
            copy.wait_recv()
        total = s2s[b][...]
        for d in range(NZ - 1):
            total = total + zrs[b][d]
        mine = pfs[b].at[core, yl]
        mine[...] = total[0:4]
        if b == 0:
            gf[core, col, yl] = total[4]
        up[b] = [copies.start(mine, mine, at(dyl=d)) for d in (3, 2, 1)]
        over[b] = [copies.start(mine, mine, at(dc=1))]
        if b == 0:
            tile = gf.at[core, col, yl]
            for dyh in (1, 0):
                for dx in (2, 1, 3, 0):
                    for dyl in (3, 2, 1, 0):
                        if dyh or dx or dyl:
                            g_out.append(copies.start(tile, tile, at(dyl=dyl, dx=dx, dyh=dyh)))

    for b in range(2):
        for d, copy in zip((3, 2, 1), up[b]):
            copy.wait_recv()
            came = pfs[b].at[core, lax.rem(yl + YL - d, YL)]
            over[b].append(copies.start(came, came, at(dc=1)))

    def products(b):
        for copy in over[b]:
            copy.wait_recv()
        pf = pfs[b]
        left = pf[:, :, 0:2].reshape(128, 128)
        right = pf[:, :, 2:4].reshape(128, 128)
        return jnp.concatenate([left, right], axis=1)

    r0 = split(dot3(split(products(0)), split(tt[:, 0].reshape(256, 256)), NN))
    c_v[...] = c_v[...] - dot3((v0h[...], v0l[...]), r0, NT)

    for copy in g_out:
        copy.wait_recv()
    g_over = copies.start(gf.at[core], gf.at[core], at(dc=1))
    g_over.wait_recv()
    gram = jnp.concatenate([gf[0].reshape(256, 128), gf[1].reshape(256, 128)], axis=1)
    moved = dot3(r0, split(gram), NT)
    rest = split(products(1) - moved)
    out_ref[...] = c_v[...] - dot3((w1h[...], w1l[...]), rest, NT)
    copies.finish()


def on_device(vectors, householder, tfactors):
    v_t = jnp.swapaxes(householder, 1, 2)
    t_t = jnp.swapaxes(tfactors, 1, 2)
    any_spec = pl.BlockSpec(memory_space=pl.ANY)
    vmem = pltpu.VMEM
    return pl.pallas_call(
        kernel,
        out_shape=jax.ShapeDtypeStruct(vectors.shape, F32),
        in_specs=[any_spec] * 3,
        out_specs=pl.BlockSpec(memory_space=pltpu.VMEM),
        scratch_shapes=[
            vmem((2, 8, 32, 512), F32),
            vmem((8, 2, 32, 256), F32),
            vmem((512, 128), F32),
            vmem((160, 512), BF16),
            vmem((160, 512), BF16),
            vmem((2, YL, 5, 8, 128), F32),
            vmem((2, YL, 4, 8, 128), F32),
            vmem((YL, 5, 8, 128), F32),
            vmem((YL, 4, 8, 128), F32),
            vmem((YL, 5, 8, 128), F32),
            vmem((YL, 4, 8, 128), F32),
            vmem((YL - 1, 5, 8, 128), F32),
            vmem((YL - 1, 4, 8, 128), F32),
            vmem((5, 8, 128), F32),
            vmem((4, 8, 128), F32),
            vmem((NZ - 1, 5, 8, 128), F32),
            vmem((NZ - 1, 4, 8, 128), F32),
            vmem((2, YL, 4, 8, 128), F32),
            vmem((2, YL, 4, 8, 128), F32),
            vmem((2, 8, YL, 8, 128), F32),
            vmem((512, 256), BF16),
            vmem((512, 256), BF16),
            vmem((512, 256), BF16),
            vmem((512, 256), BF16),
            pltpu.SemaphoreType.DMA((4,)),
            pltpu.SemaphoreType.DMA((N_COPIES,)),
            pltpu.SemaphoreType.DMA((N_COPIES,)),
        ],
        compiler_params=pltpu.CompilerParams(
            collective_id=0, has_side_effects=True, vmem_limit_bytes=60 * 2**20
        ),
        cost_estimate=pl.CostEstimate(flops=500_000_000, bytes_accessed=2_000_000, transcendentals=0),
        name="reflect",
    )(v_t, t_t, vectors)


def solution(mesh):
    return jax.shard_map(
        on_device,
        mesh=mesh,
        in_specs=(P("row", "col"), P(None, "row", "col"), P(None, None, "col")),
        out_specs=P("row", "col"),
        check_vma=False,
    )
```

```python
import functools

import jax
import jax.numpy as jnp
from jax import lax
from jax.experimental import pallas as pl
from jax.experimental.pallas import tpu as pltpu
from jax.sharding import PartitionSpec as P

MESH = pl.DeviceIdType.MESH
F32 = jnp.float32
BF16 = jnp.bfloat16
YL, NZ, CORES = 4, 8, 2
YH, NX = 2, 4
NT = (((1,), (1,)), ((), ()))
NN = (((1,), (0,)), ((), ()))


def split(value):
    high = value.astype(BF16)
    return high, (value - high.astype(F32)).astype(BF16)


def dot3(a, b, dims):
    def one(left, right):
        return lax.dot_general(left, right, dims, preferred_element_type=F32)

    return one(a[0], b[0]) + (one(a[0], b[1]) + one(a[1], b[0]))


class Copies:
    def __init__(self, send, recv):
        self.send, self.recv, self.used, self.open = send, recv, 0, []

    def start(self, src, dst, device):
        at = self.used
        self.used += 1
        copy = pltpu.make_async_remote_copy(
            src_ref=src,
            dst_ref=dst,
            send_sem=self.send.at[at],
            recv_sem=self.recv.at[at],
            device_id=device,
            device_id_type=MESH,
        )
        copy.start()
        self.open.append(copy)
        return copy

    def finish(self):
        for copy in self.open:
            copy.wait_send()


N_COPIES = 114
Z_ORDER = (4, 3, 5, 2, 6, 1, 7)
OTHERS = tuple((dyl, dc) for dyl in (3, 2, 1, 0) for dc in (1, 0) if dyl or dc)
NEAR, FAR = 0, 1
SETS = (((0, NEAR), (1, NEAR)), ((0, FAR),), ((1, FAR),))
DIRECT = (False, True, True)


def kernel(sets, direct, v_in, t_in, c_in, out_ref, *scratch):
    (
        vt, tt, c_v, lhs_h, lhs_l, w1h, w1l, v0h, v0l, r0h, r0l, gf, local_sem, send_sem, recv_sem,
    ), per_set = scratch[:15], scratch[15:]
    parts = [per_set[7 * i : 7 * i + 7] for i in range(len(sets))]
    row, col = lax.axis_index("row"), lax.axis_index("col")
    core, z, yl = lax.rem(row, 2), lax.rem(row // 2, NZ), row // (2 * NZ)
    x, yh = lax.rem(col, NX), col // NX
    cores = [core, 1 - core]
    zs = [lax.rem(z + d, NZ) for d in range(NZ)]
    yls = [lax.rem(yl + d, YL) for d in range(YL)]
    xs = [lax.rem(x + d, NX) for d in range(NX)]
    halves = [yh, 1 - yh]
    other_col = halves[FAR] * NX + x

    def at(dc=0, dz=0, dyl=0, dx=0, dyh=0):
        return (yls[dyl] * (2 * NZ) + zs[dz] * 2 + cores[dc], halves[dyh] * NX + xs[dx])

    load_v = [pltpu.make_async_copy(v_in.at[b], vt.at[b, col], local_sem.at[b]) for b in range(2)]
    load_c = pltpu.make_async_copy(c_in, c_v, local_sem.at[2])
    load_t = pltpu.make_async_copy(t_in.at[core], tt.at[core, col], local_sem.at[3])
    for load in (*load_v, load_c, load_t):
        load.start()

    barrier = pltpu.get_barrier_semaphore()
    partners = [at(dyh=1)] + [at(dx=d) for d in (2, 1, 3)] + [at(dz=d) for d in Z_ORDER]
    partners += [at(dyl=dyl, dc=dc) for dyl, dc in OTHERS]
    for device in partners:
        pl.semaphore_signal(barrier, inc=1, device_id=device, device_id_type=MESH)
    for load in load_v:
        load.wait()
    pl.semaphore_wait(barrier, len(partners))

    copies = Copies(send_sem, recv_sem)
    going = {}

    def wait(*names):
        for name in names:
            for copy in going.pop(name, ()):
                copy.wait_recv()

    def along_x(ref):
        return [copies.start(ref, ref, at(dx=d)) for d in (2, 1, 3)]

    def to_partner(ref):
        return [copies.start(ref, ref, at(dyh=1))]

    def send_x0():
        going["x0"] = along_x(vt.at[0, col])

    def send_x1():
        going["x1"] = along_x(vt.at[1, col])

    def send_y0():
        going["y0"] = to_partner(vt.at[0, col])

    def send_y1():
        going["y1"] = to_partner(vt.at[1, col])

    def send_yt():
        load_t.wait()
        going["yt"] = to_partner(tt.at[core, col])

    def turn_own():
        load_c.wait()
        for part in range(2):
            high, low = split(jnp.transpose(c_v[pl.ds(256 * part, 256), :]))
            lhs_h[0:128, 256 * part : 256 * (part + 1)] = high
            lhs_l[0:128, 256 * part : 256 * (part + 1)] = low

    def relay0():
        wait("y0")
        going["r0"] = along_x(vt.at[0, other_col])

    def relay1():
        wait("y1")
        going["r1"] = along_x(vt.at[1, other_col])

    def gram_rows():
        for half in range(2):
            first = 128 + 32 * half
            high, low = split(vt[1, half * NX + x])
            lhs_h[first : first + 32, :] = high
            lhs_l[first : first + 32, :] = low

    def relay_t():
        wait("yt")
        going["rt"] = along_x(tt.at[core, col]) + along_x(tt.at[core, other_col])

    def swap_t():
        wait("rt")
        going["ct"] = [copies.start(tt.at[core], tt.at[core], at(dc=1))]

    def mul(i):
        pp, rs = parts[i][:2]
        grams = 2 * len(sets[i])
        for n, (b, half) in enumerate(sets[i]):
            wait(("x0", "x1")[b] if half == NEAR else ("r0", "r1")[b])
            rows = 192 if (b, half) == (0, NEAR) else 128
            blockv = split(vt[b, pl.ds(halves[half] * NX, NX)].reshape(128, 512))
            value = dot3((lhs_h[0:rows, :], lhs_l[0:rows, :]), blockv, NT)
            for e in range(2 * YL):
                c, y = divmod(e, YL)
                pp[c, y, 2 * n : 2 * n + 2] = value[16 * e : 16 * e + 16].reshape(2, 8, 128)
                if rows == 192:
                    pp[c, y, grams] = value[128 + 8 * e : 136 + 8 * e]
        if direct[i]:
            going["y", i] = [
                copies.start(pp.at[cores[dc], yls[dyl]], parts[i][3].at[j], at(dyl=dyl, dc=dc))
                for j, (dyl, dc) in enumerate(OTHERS)
            ]
        else:
            going["core", i] = [copies.start(pp.at[1 - core], rs, at(dc=1))]

    def down(i):
        if direct[i]:
            return
        pp, rs, held, yr, _, _, _ = parts[i]
        wait(("core", i))
        held[...] = pp[core] + rs[...]
        going["y", i] = [
            copies.start(held.at[yls[d]], yr.at[d - 1], at(dyl=d)) for d in (3, 2, 1)
        ]

    def around(i):
        pp, _, held, yr, mine, zr, _ = parts[i]
        wait(("y", i))
        if direct[i]:
            total = pp[core, yl]
            for j in range(len(OTHERS)):
                total = total + yr[j]
            mine[...] = total
        else:
            mine[...] = held[yl] + yr[0] + (yr[1] + yr[2])
        going["z", i] = [copies.start(mine, zr.at[d - 1], at(dz=d)) for d in Z_ORDER]

    def up(i):
        mine, zr, pf = parts[i][4:]
        wait(("z", i))
        total = mine[...]
        for d in range(NZ - 1):
            total = total + zr[d]
        grams = 2 * len(sets[i])
        pf[core, yl] = total[0:grams]
        sent = pf.at[core, yl]
        if direct[i]:
            going["over", i] = [copies.start(sent, sent, at(dyl=dyl, dc=dc)) for dyl, dc in OTHERS]
        else:
            going["up", i] = [copies.start(sent, sent, at(dyl=d)) for d in (3, 2, 1)]
            going["over", i] = [copies.start(sent, sent, at(dc=1))]
        if (0, NEAR) in sets[i]:
            gf[core, yh, x, yl] = total[grams]
            place = gf.at[core, yh, x, yl]
            going["g"] = [
                copies.start(place, place, at(dx=dx, dyl=dyl, dyh=dyh))
                for dyh in (1, 0)
                for dyl in (3, 2, 1, 0)
                for dx in (2, 1, 3, 0)
                if dx or dyl or dyh
            ]

    def over(i):
        if direct[i]:
            return
        pf = parts[i][6]
        for d, copy in zip((3, 2, 1), going.pop(("up", i))):
            copy.wait_recv()
            came = pf.at[core, lax.rem(yl + YL - d, YL)]
            going["over", i].append(copies.start(came, came, at(dc=1)))

    def pre0():
        wait("r0")
        for half in range(2):
            block = vt[0, pl.ds(halves[half] * NX, NX)].reshape(128, 512)
            high, low = split(jnp.transpose(block))
            v0h[:, 128 * half : 128 * (half + 1)] = high
            v0l[:, 128 * half : 128 * (half + 1)] = low

    def factor(b):
        both = [tt[b, pl.ds(half * NX, NX)].reshape(128, 256) for half in halves]
        return split(jnp.concatenate(both, axis=0))

    def pre1():
        wait("r1", "ct")
        v1 = split(jnp.transpose(vt[1].reshape(256, 512)))
        w1h[...], w1l[...] = split(dot3(v1, factor(1), NT))

    def products(b):
        found = {}
        for i, pieces in enumerate(sets):
            for n, piece in enumerate(pieces):
                found[piece] = parts[i][6][:, :, 2 * n : 2 * n + 2].reshape(128, 128)
        return jnp.concatenate([found[b, NEAR], found[b, FAR]], axis=1)

    def gram_over():
        wait("g")
        going["gc"] = [copies.start(gf.at[core], gf.at[core], at(dc=1))]

    def gram(half):
        tiles = [gf[k1, halves[half], g].reshape(32, 128) for k1 in halves for g in range(NX)]
        return jnp.concatenate(tiles, axis=0)

    def last():
        wait(*(("over", i) for i in range(len(sets)) if any(b == 0 for b, _ in sets[i])))
        high, low = split(dot3(split(products(0)), factor(0), NN))
        for h in range(2):
            r0h[h] = high[:, 128 * h : 128 * (h + 1)]
            r0l[h] = low[:, 128 * h : 128 * (h + 1)]
        r0 = tuple(jnp.concatenate([r[half] for half in halves], axis=1) for r in (r0h, r0l))
        c_v[...] = c_v[...] - dot3((v0h[...], v0l[...]), r0, NT)
        wait("gc")
        moved = dot3(r0, split(jnp.concatenate([gram(0), gram(1)], axis=1)), NT)
        wait(*(("over", i) for i in range(len(sets))))
        rest = split(products(1) - moved)
        out_ref[...] = c_v[...] - dot3((w1h[...], w1l[...]), rest, NT)

    send_y0()
    send_x0()
    send_y1()
    send_x1()
    send_yt()
    turn_own()
    relay0()
    relay1()
    gram_rows()
    mul(0)
    down(0)
    mul(1)
    around(0)
    mul(2)
    around(1)
    relay_t()
    up(0)
    around(2)
    pre0()
    up(1)
    over(0)
    up(2)
    swap_t()
    pre1()
    gram_over()
    last()
    copies.finish()


def on_device(vectors, householder, tfactors):
    v_t = jnp.swapaxes(householder, 1, 2)
    t_t = jnp.swapaxes(tfactors, 1, 2)
    anywhere = pl.BlockSpec(memory_space=pl.ANY)
    vmem = pltpu.VMEM
    tiles = lambda *shape: vmem((*shape, 8, 128), F32)
    scratch = [
        vmem((2, 8, 32, 512), F32),
        vmem((2, 8, 32, 256), F32),
        vmem((512, 128), F32),
        vmem((192, 512), BF16),
        vmem((192, 512), BF16),
        vmem((512, 256), BF16),
        vmem((512, 256), BF16),
        vmem((512, 256), BF16),
        vmem((512, 256), BF16),
        vmem((2, 128, 128), BF16),
        vmem((2, 128, 128), BF16),
        tiles(2, 2, NX, YL),
        pltpu.SemaphoreType.DMA((4,)),
        pltpu.SemaphoreType.DMA((N_COPIES,)),
        pltpu.SemaphoreType.DMA((N_COPIES,)),
    ]
    for pieces in SETS:
        n = 2 * len(pieces)
        with_gram = n + ((0, NEAR) in pieces)
        scratch += [
            tiles(2, YL, with_gram), tiles(YL, with_gram), tiles(YL, with_gram), tiles(7, with_gram),
            tiles(with_gram), tiles(NZ - 1, with_gram), tiles(2, YL, n),
        ]
    return pl.pallas_call(
        functools.partial(kernel, SETS, DIRECT),
        out_shape=pltpu.VMEM(vectors.shape, F32),
        in_specs=[anywhere] * 3,
        out_specs=pl.BlockSpec(memory_space=pltpu.VMEM),
        scratch_shapes=scratch,
        compiler_params=pltpu.CompilerParams(
            collective_id=0, has_side_effects=True, vmem_limit_bytes=61440 * 1024
        ),
        cost_estimate=pl.CostEstimate(flops=500_000_000, bytes_accessed=2_000_000, transcendentals=0),
        name="reflect",
    )(v_t, t_t, vectors)


def solution(mesh):
    return jax.shard_map(
        on_device,
        mesh=mesh,
        in_specs=(P("row", "col"), P(None, "row", "col"), P(None, None, "col")),
        out_specs=P("row", "col"),
        check_vma=False,
    )
```

```python
import functools

import jax
import jax.numpy as jnp
from jax import lax
from jax.experimental import pallas as pl
from jax.experimental.pallas import tpu as pltpu
from jax.sharding import PartitionSpec as P

MESH = pl.DeviceIdType.MESH
F32 = jnp.float32
BF16 = jnp.bfloat16
YL, NZ, CORES = 4, 8, 2
YH, NX = 2, 4
NT = (((1,), (1,)), ((), ()))
NN = (((1,), (0,)), ((), ()))


def split(value):
    high = value.astype(BF16)
    return high, (value - high.astype(F32)).astype(BF16)


def dot3(a, b, dims):
    def one(left, right):
        return lax.dot_general(left, right, dims, preferred_element_type=F32)

    return one(a[0], b[0]) + (one(a[0], b[1]) + one(a[1], b[0]))


class Copies:
    def __init__(self, send, recv):
        self.send, self.recv, self.used, self.open = send, recv, 0, []

    def start(self, src, dst, device):
        at = self.used
        self.used += 1
        copy = pltpu.make_async_remote_copy(
            src_ref=src,
            dst_ref=dst,
            send_sem=self.send.at[at],
            recv_sem=self.recv.at[at],
            device_id=device,
            device_id_type=MESH,
        )
        copy.start()
        self.open.append(copy)
        return copy

    def finish(self):
        for copy in self.open:
            copy.wait_send()


N_COPIES = 138
Z_ORDER = (4, 3, 5, 2, 6, 1, 7)
OTHERS = tuple((dyl, dc) for dyl in (3, 2, 1, 0) for dc in (1, 0) if dyl or dc)
NEAR, FAR = 0, 1
GRAM = (1, NEAR)
SETS = (((0, NEAR),), ((1, NEAR),), ((0, FAR),), ((1, FAR),))
DIRECT = (True, True, True, True)


def kernel(sets, direct, v_in, t_in, c_in, out_ref, *scratch):
    (
        vt, tt, c_v, lhs_h, lhs_l, w1h, w1l, v0h, v0l, r0h, r0l, gf, local_sem, send_sem, recv_sem,
    ), per_set = scratch[:15], scratch[15:]
    parts = [per_set[7 * i : 7 * i + 7] for i in range(len(sets))]
    row, col = lax.axis_index("row"), lax.axis_index("col")
    core, z, yl = lax.rem(row, 2), lax.rem(row // 2, NZ), row // (2 * NZ)
    x, yh = lax.rem(col, NX), col // NX
    cores = [core, 1 - core]
    zs = [lax.rem(z + d, NZ) for d in range(NZ)]
    yls = [lax.rem(yl + d, YL) for d in range(YL)]
    xs = [lax.rem(x + d, NX) for d in range(NX)]
    halves = [yh, 1 - yh]
    other_col = halves[FAR] * NX + x

    def at(dc=0, dz=0, dyl=0, dx=0, dyh=0):
        return (yls[dyl] * (2 * NZ) + zs[dz] * 2 + cores[dc], halves[dyh] * NX + xs[dx])

    load_v = [pltpu.make_async_copy(v_in.at[b], vt.at[b, col], local_sem.at[b]) for b in range(2)]
    load_c = pltpu.make_async_copy(c_in, c_v, local_sem.at[2])
    load_t = pltpu.make_async_copy(t_in.at[core], tt.at[core, col], local_sem.at[3])
    for load in (*load_v, load_c, load_t):
        load.start()

    barrier = pltpu.get_barrier_semaphore()
    partners = [at(dyh=1)] + [at(dx=d) for d in (2, 1, 3)] + [at(dz=d) for d in Z_ORDER]
    partners += [at(dyl=dyl, dc=dc) for dyl, dc in OTHERS]
    for device in partners:
        pl.semaphore_signal(barrier, inc=1, device_id=device, device_id_type=MESH)
    for load in load_v:
        load.wait()
    pl.semaphore_wait(barrier, len(partners))

    copies = Copies(send_sem, recv_sem)
    going = {}

    def wait(*names):
        for name in names:
            for copy in going.pop(name, ()):
                copy.wait_recv()

    def along_x(ref):
        return [copies.start(ref, ref, at(dx=d)) for d in (2, 1, 3)]

    def to_partner(ref):
        return [copies.start(ref, ref, at(dyh=1))]

    def send_x0():
        going["x0"] = along_x(vt.at[0, col])

    def send_x1():
        going["x1"] = along_x(vt.at[1, col])

    def send_y0():
        going["y0"] = to_partner(vt.at[0, col])

    def send_y1():
        going["y1"] = to_partner(vt.at[1, col])

    def send_yt():
        load_t.wait()
        going["yt"] = to_partner(tt.at[core, col])

    def turn_own():
        load_c.wait()
        for part in range(2):
            high, low = split(jnp.transpose(c_v[pl.ds(256 * part, 256), :]))
            lhs_h[0:128, 256 * part : 256 * (part + 1)] = high
            lhs_l[0:128, 256 * part : 256 * (part + 1)] = low

    def relay0():
        wait("y0")
        going["r0"] = along_x(vt.at[0, other_col])

    def relay1():
        wait("y1")
        going["r1"] = along_x(vt.at[1, other_col])

    def gram_rows():
        for half in range(2):
            first = 128 + 32 * half
            high, low = split(vt[1, half * NX + x])
            lhs_h[first : first + 32, :] = high
            lhs_l[first : first + 32, :] = low

    def relay_t():
        wait("yt")
        going["rt"] = along_x(tt.at[core, col]) + along_x(tt.at[core, other_col])

    def swap_t():
        wait("rt")
        going["ct"] = [copies.start(tt.at[core], tt.at[core], at(dc=1))]

    def mul(i):
        pp, rs = parts[i][:2]
        grams = 2 * len(sets[i])
        for n, (b, half) in enumerate(sets[i]):
            wait(("x0", "x1")[b] if half == NEAR else ("r0", "r1")[b])
            blockv = split(vt[b, pl.ds(halves[half] * NX, NX)].reshape(128, 512))
            value = dot3((lhs_h[0:128, :], lhs_l[0:128, :]), blockv, NT)
            for e in range(2 * YL):
                c, y = divmod(e, YL)
                pp[c, y, 2 * n : 2 * n + 2] = value[16 * e : 16 * e + 16].reshape(2, 8, 128)
        if GRAM in sets[i]:
            wait("x0")
            blockv = split(vt[0, pl.ds(yh * NX, NX)].reshape(128, 512))
            value = dot3((lhs_h[128:192, :], lhs_l[128:192, :]), blockv, NT)
            for e in range(2 * YL):
                c, y = divmod(e, YL)
                pp[c, y, grams] = value[8 * e : 8 * e + 8]
        if direct[i]:
            going["y", i] = [
                copies.start(pp.at[cores[dc], yls[dyl]], parts[i][3].at[j], at(dyl=dyl, dc=dc))
                for j, (dyl, dc) in enumerate(OTHERS)
            ]
        else:
            going["core", i] = [copies.start(pp.at[1 - core], rs, at(dc=1))]

    def down(i):
        if direct[i]:
            return
        pp, rs, held, yr, _, _, _ = parts[i]
        wait(("core", i))
        held[...] = pp[core] + rs[...]
        going["y", i] = [
            copies.start(held.at[yls[d]], yr.at[d - 1], at(dyl=d)) for d in (3, 2, 1)
        ]

    def around(i):
        pp, _, held, yr, mine, zr, _ = parts[i]
        wait(("y", i))
        if direct[i]:
            total = pp[core, yl]
            for j in range(len(OTHERS)):
                total = total + yr[j]
            mine[...] = total
        else:
            mine[...] = held[yl] + yr[0] + (yr[1] + yr[2])
        going["z", i] = [copies.start(mine, zr.at[d - 1], at(dz=d)) for d in Z_ORDER]

    def up(i):
        mine, zr, pf = parts[i][4:]
        wait(("z", i))
        total = mine[...]
        for d in range(NZ - 1):
            total = total + zr[d]
        grams = 2 * len(sets[i])
        pf[core, yl] = total[0:grams]
        sent = pf.at[core, yl]
        if direct[i]:
            going["over", i] = [copies.start(sent, sent, at(dyl=dyl, dc=dc)) for dyl, dc in OTHERS]
        else:
            going["up", i] = [copies.start(sent, sent, at(dyl=d)) for d in (3, 2, 1)]
            going["over", i] = [copies.start(sent, sent, at(dc=1))]
        if GRAM in sets[i]:
            gf[core, yh, x, yl] = total[grams]
            place = gf.at[core, yh, x, yl]
            going["g"] = [
                copies.start(place, place, at(dx=dx, dyl=dyl, dyh=dyh))
                for dyh in (1, 0)
                for dyl in (3, 2, 1, 0)
                for dx in (2, 1, 3, 0)
                if dx or dyl or dyh
            ]

    def over(i):
        if direct[i]:
            return
        pf = parts[i][6]
        for d, copy in zip((3, 2, 1), going.pop(("up", i))):
            copy.wait_recv()
            came = pf.at[core, lax.rem(yl + YL - d, YL)]
            going["over", i].append(copies.start(came, came, at(dc=1)))

    def pre0():
        wait("r0")
        for half in range(2):
            block = vt[0, pl.ds(halves[half] * NX, NX)].reshape(128, 512)
            high, low = split(jnp.transpose(block))
            v0h[:, 128 * half : 128 * (half + 1)] = high
            v0l[:, 128 * half : 128 * (half + 1)] = low

    def factor(b):
        both = [tt[b, pl.ds(half * NX, NX)].reshape(128, 256) for half in halves]
        return split(jnp.concatenate(both, axis=0))

    def pre1():
        wait("r1", "ct")
        v1 = split(jnp.transpose(vt[1].reshape(256, 512)))
        w1h[...], w1l[...] = split(dot3(v1, factor(1), NT))

    def products(b):
        found = {}
        for i, pieces in enumerate(sets):
            for n, piece in enumerate(pieces):
                found[piece] = parts[i][6][:, :, 2 * n : 2 * n + 2].reshape(128, 128)
        return jnp.concatenate([found[b, NEAR], found[b, FAR]], axis=1)

    def gram_over():
        wait("g")
        going["gc"] = [copies.start(gf.at[core], gf.at[core], at(dc=1))]

    def gram(half):
        tiles = [gf[k1, halves[half], g].reshape(32, 128) for k1 in halves for g in range(NX)]
        return jnp.concatenate(tiles, axis=0)

    def last():
        wait(*(("over", i) for i in range(len(sets)) if any(b == 0 for b, _ in sets[i])))
        high, low = split(dot3(split(products(0)), factor(0), NN))
        for h in range(2):
            r0h[h] = high[:, 128 * h : 128 * (h + 1)]
            r0l[h] = low[:, 128 * h : 128 * (h + 1)]
        r0 = tuple(jnp.concatenate([r[half] for half in halves], axis=1) for r in (r0h, r0l))
        c_v[...] = c_v[...] - dot3((v0h[...], v0l[...]), r0, NT)
        wait("gc")
        moved = dot3(r0, split(jnp.concatenate([gram(0), gram(1)], axis=1)), NT)
        wait(*(("over", i) for i in range(len(sets))))
        rest = split(products(1) - moved)
        out_ref[...] = c_v[...] - dot3((w1h[...], w1l[...]), rest, NT)

    send_y0()
    send_x0()
    send_y1()
    send_x1()
    send_yt()
    turn_own()
    relay0()
    mul(0)
    relay1()
    gram_rows()
    mul(1)
    around(0)
    mul(2)
    around(1)
    mul(3)
    up(0)
    around(2)
    relay_t()
    up(1)
    around(3)
    pre0()
    up(2)
    swap_t()
    pre1()
    up(3)
    gram_over()
    last()
    copies.finish()


def on_device(vectors, householder, tfactors):
    v_t = jnp.swapaxes(householder, 1, 2)
    t_t = jnp.swapaxes(tfactors, 1, 2)
    anywhere = pl.BlockSpec(memory_space=pl.ANY)
    vmem = pltpu.VMEM
    tiles = lambda *shape: vmem((*shape, 8, 128), F32)
    scratch = [
        vmem((2, 8, 32, 512), F32),
        vmem((2, 8, 32, 256), F32),
        vmem((512, 128), F32),
        vmem((192, 512), BF16),
        vmem((192, 512), BF16),
        vmem((512, 256), BF16),
        vmem((512, 256), BF16),
        vmem((512, 256), BF16),
        vmem((512, 256), BF16),
        vmem((2, 128, 128), BF16),
        vmem((2, 128, 128), BF16),
        tiles(2, 2, NX, YL),
        pltpu.SemaphoreType.DMA((4,)),
        pltpu.SemaphoreType.DMA((N_COPIES,)),
        pltpu.SemaphoreType.DMA((N_COPIES,)),
    ]
    for pieces in SETS:
        n = 2 * len(pieces)
        with_gram = n + (GRAM in pieces)
        scratch += [
            tiles(2, YL, with_gram), tiles(YL, with_gram), tiles(YL, with_gram), tiles(7, with_gram),
            tiles(with_gram), tiles(NZ - 1, with_gram), tiles(2, YL, n),
        ]
    return pl.pallas_call(
        functools.partial(kernel, SETS, DIRECT),
        out_shape=pltpu.VMEM(vectors.shape, F32),
        in_specs=[anywhere] * 3,
        out_specs=pl.BlockSpec(memory_space=pltpu.VMEM),
        scratch_shapes=scratch,
        compiler_params=pltpu.CompilerParams(
            collective_id=0, has_side_effects=True, vmem_limit_bytes=60 * 2**20
        ),
        cost_estimate=pl.CostEstimate(flops=500_000_000, bytes_accessed=2_000_000, transcendentals=0),
        name="reflect",
    )(v_t, t_t, vectors)


def solution(mesh):
    return jax.shard_map(
        on_device,
        mesh=mesh,
        in_specs=(P("row", "col"), P(None, "row", "col"), P(None, None, "col")),
        out_specs=P("row", "col"),
        check_vma=False,
    )
```

```python
import functools

import jax
import jax.numpy as jnp
from jax import lax
from jax.experimental import pallas as pl
from jax.experimental.pallas import tpu as pltpu
from jax.sharding import PartitionSpec as P

MESH = pl.DeviceIdType.MESH
F32 = jnp.float32
BF16 = jnp.bfloat16
YL, NZ, CORES = 4, 8, 2
YH, NX = 2, 4
NT = (((1,), (1,)), ((), ()))
NN = (((1,), (0,)), ((), ()))


def split(value):
    high = value.astype(BF16)
    return high, (value - high.astype(F32)).astype(BF16)


def dot3(a, b, dims):
    def one(left, right):
        return lax.dot_general(left, right, dims, preferred_element_type=F32)

    return one(a[0], b[0]) + (one(a[0], b[1]) + one(a[1], b[0]))


class Copies:
    def __init__(self, send, recv):
        self.send, self.recv, self.used, self.open = send, recv, 0, []

    def start(self, src, dst, device):
        at = self.used
        self.used += 1
        copy = pltpu.make_async_remote_copy(
            src_ref=src,
            dst_ref=dst,
            send_sem=self.send.at[at],
            recv_sem=self.recv.at[at],
            device_id=device,
            device_id_type=MESH,
        )
        copy.start()
        self.open.append(copy)
        return copy

    def finish(self):
        for copy in self.open:
            copy.wait_send()


N_COPIES = 138
Z_ORDER = (4, 3, 5, 2, 6, 1, 7)
OTHERS = tuple((dyl, dc) for dyl in (3, 2, 1, 0) for dc in (1, 0) if dyl or dc)
NEAR, FAR = 0, 1
GRAM = (1, NEAR)
SETS = (((0, NEAR),), ((1, NEAR),), ((0, FAR),), ((1, FAR),))
DIRECT = (True, True, True, True)


def kernel(sets, direct, v_in, t_in, c_in, out_ref, *scratch):
    (
        vt, tt, c_v, lhs_h, lhs_l, w1h, w1l, v0h, v0l, r0h, r0l, gf, local_sem, send_sem, recv_sem,
    ), per_set = scratch[:15], scratch[15:]
    parts = [per_set[7 * i : 7 * i + 7] for i in range(len(sets))]
    row, col = lax.axis_index("row"), lax.axis_index("col")
    core, z, yl = lax.rem(row, 2), lax.rem(row // 2, NZ), row // (2 * NZ)
    x, yh = lax.rem(col, NX), col // NX
    cores = [core, 1 - core]
    zs = [lax.rem(z + d, NZ) for d in range(NZ)]
    yls = [lax.rem(yl + d, YL) for d in range(YL)]
    xs = [lax.rem(x + d, NX) for d in range(NX)]
    halves = [yh, 1 - yh]
    other_col = halves[FAR] * NX + x

    def at(dc=0, dz=0, dyl=0, dx=0, dyh=0):
        return (yls[dyl] * (2 * NZ) + zs[dz] * 2 + cores[dc], halves[dyh] * NX + xs[dx])

    load_v = [pltpu.make_async_copy(v_in.at[b], vt.at[b, col], local_sem.at[b]) for b in range(2)]
    load_c = pltpu.make_async_copy(c_in, c_v, local_sem.at[2])
    load_t = pltpu.make_async_copy(t_in.at[core], tt.at[core, col], local_sem.at[3])
    for load in (*load_v, load_c, load_t):
        load.start()

    barrier = pltpu.get_barrier_semaphore()
    partners = [at(dyh=1)] + [at(dx=d) for d in (2, 1, 3)] + [at(dz=d) for d in Z_ORDER]
    partners += [at(dyl=dyl, dc=dc) for dyl, dc in OTHERS]
    for device in partners:
        pl.semaphore_signal(barrier, inc=1, device_id=device, device_id_type=MESH)
    for load in load_v:
        load.wait()
    pl.semaphore_wait(barrier, len(partners))

    copies = Copies(send_sem, recv_sem)
    going = {}

    def wait(*names):
        for name in names:
            for copy in going.pop(name, ()):
                copy.wait_recv()

    def along_x(ref):
        return [copies.start(ref, ref, at(dx=d)) for d in (1, 3, 2)]

    def to_partner(ref):
        return [copies.start(ref, ref, at(dyh=1))]

    def send_x0():
        going["x0"] = along_x(vt.at[0, col])

    def send_x1():
        going["x1"] = along_x(vt.at[1, col])

    def send_y0():
        going["y0"] = to_partner(vt.at[0, col])

    def send_y1():
        going["y1"] = to_partner(vt.at[1, col])

    def send_yt():
        load_t.wait()
        going["yt"] = to_partner(tt.at[core, col])

    def turn_own():
        load_c.wait()
        for part in range(2):
            high, low = split(jnp.transpose(c_v[pl.ds(256 * part, 256), :]))
            lhs_h[0:128, 256 * part : 256 * (part + 1)] = high
            lhs_l[0:128, 256 * part : 256 * (part + 1)] = low

    def relay0():
        wait("y0")
        going["r0"] = along_x(vt.at[0, other_col])

    def relay1():
        wait("y1")
        going["r1"] = along_x(vt.at[1, other_col])

    def gram_rows():
        for half in range(2):
            first = 128 + 32 * half
            high, low = split(vt[1, half * NX + x])
            lhs_h[first : first + 32, :] = high
            lhs_l[first : first + 32, :] = low

    def relay_t():
        wait("yt")
        going["rt"] = along_x(tt.at[core, col]) + along_x(tt.at[core, other_col])

    def swap_t():
        wait("rt")
        going["ct"] = [copies.start(tt.at[core], tt.at[core], at(dc=1))]

    def mul(i):
        pp, rs = parts[i][:2]
        grams = 2 * len(sets[i])
        for n, (b, half) in enumerate(sets[i]):
            wait(("x0", "x1")[b] if half == NEAR else ("r0", "r1")[b])
            blockv = split(vt[b, pl.ds(halves[half] * NX, NX)].reshape(128, 512))
            value = dot3((lhs_h[0:128, :], lhs_l[0:128, :]), blockv, NT)
            for e in range(2 * YL):
                c, y = divmod(e, YL)
                pp[c, y, 2 * n : 2 * n + 2] = value[16 * e : 16 * e + 16].reshape(2, 8, 128)
        if GRAM in sets[i]:
            wait("x0")
            blockv = split(vt[0, pl.ds(yh * NX, NX)].reshape(128, 512))
            value = dot3((lhs_h[128:192, :], lhs_l[128:192, :]), blockv, NT)
            for e in range(2 * YL):
                c, y = divmod(e, YL)
                pp[c, y, grams] = value[8 * e : 8 * e + 8]
        if direct[i]:
            going["y", i] = [
                copies.start(pp.at[cores[dc], yls[dyl]], parts[i][3].at[j], at(dyl=dyl, dc=dc))
                for j, (dyl, dc) in enumerate(OTHERS)
            ]
        else:
            going["core", i] = [copies.start(pp.at[1 - core], rs, at(dc=1))]

    def down(i):
        if direct[i]:
            return
        pp, rs, held, yr, _, _, _ = parts[i]
        wait(("core", i))
        held[...] = pp[core] + rs[...]
        going["y", i] = [
            copies.start(held.at[yls[d]], yr.at[d - 1], at(dyl=d)) for d in (3, 2, 1)
        ]

    def around(i):
        pp, _, held, yr, mine, zr, _ = parts[i]
        wait(("y", i))
        if direct[i]:
            total = pp[core, yl]
            for j in range(len(OTHERS)):
                total = total + yr[j]
            mine[...] = total
        else:
            mine[...] = held[yl] + yr[0] + (yr[1] + yr[2])
        going["z", i] = [copies.start(mine, zr.at[d - 1], at(dz=d)) for d in Z_ORDER]

    def up(i):
        mine, zr, pf = parts[i][4:]
        wait(("z", i))
        total = mine[...]
        for d in range(NZ - 1):
            total = total + zr[d]
        grams = 2 * len(sets[i])
        pf[core, yl] = total[0:grams]
        sent = pf.at[core, yl]
        if direct[i]:
            going["over", i] = [copies.start(sent, sent, at(dyl=dyl, dc=dc)) for dyl, dc in OTHERS]
        else:
            going["up", i] = [copies.start(sent, sent, at(dyl=d)) for d in (3, 2, 1)]
            going["over", i] = [copies.start(sent, sent, at(dc=1))]
        if GRAM in sets[i]:
            gf[core, yh, x, yl] = total[grams]
            place = gf.at[core, yh, x, yl]
            going["g"] = [
                copies.start(place, place, at(dx=dx, dyl=dyl, dyh=dyh))
                for dyh in (1, 0)
                for dyl in (3, 2, 1, 0)
                for dx in (2, 1, 3, 0)
                if dx or dyl or dyh
            ]

    def over(i):
        if direct[i]:
            return
        pf = parts[i][6]
        for d, copy in zip((3, 2, 1), going.pop(("up", i))):
            copy.wait_recv()
            came = pf.at[core, lax.rem(yl + YL - d, YL)]
            going["over", i].append(copies.start(came, came, at(dc=1)))

    def pre0():
        wait("r0")
        for half in range(2):
            block = vt[0, pl.ds(halves[half] * NX, NX)].reshape(128, 512)
            high, low = split(jnp.transpose(block))
            v0h[:, 128 * half : 128 * (half + 1)] = high
            v0l[:, 128 * half : 128 * (half + 1)] = low

    def factor(b):
        both = [tt[b, pl.ds(half * NX, NX)].reshape(128, 256) for half in halves]
        return split(jnp.concatenate(both, axis=0))

    def pre1():
        wait("r1", "ct")
        v1 = split(jnp.transpose(vt[1].reshape(256, 512)))
        w1h[...], w1l[...] = split(dot3(v1, factor(1), NT))

    def products(b):
        found = {}
        for i, pieces in enumerate(sets):
            for n, piece in enumerate(pieces):
                found[piece] = parts[i][6][:, :, 2 * n : 2 * n + 2].reshape(128, 128)
        return jnp.concatenate([found[b, NEAR], found[b, FAR]], axis=1)

    def gram_over():
        wait("g")
        going["gc"] = [copies.start(gf.at[core], gf.at[core], at(dc=1))]

    def gram(half):
        tiles = [gf[k1, halves[half], g].reshape(32, 128) for k1 in halves for g in range(NX)]
        return jnp.concatenate(tiles, axis=0)

    def last():
        wait(*(("over", i) for i in range(len(sets)) if any(b == 0 for b, _ in sets[i])))
        high, low = split(dot3(split(products(0)), factor(0), NN))
        for h in range(2):
            r0h[h] = high[:, 128 * h : 128 * (h + 1)]
            r0l[h] = low[:, 128 * h : 128 * (h + 1)]
        r0 = tuple(jnp.concatenate([r[half] for half in halves], axis=1) for r in (r0h, r0l))
        c_v[...] = c_v[...] - dot3((v0h[...], v0l[...]), r0, NT)
        wait("gc")
        moved = dot3(r0, split(jnp.concatenate([gram(0), gram(1)], axis=1)), NT)
        wait(*(("over", i) for i in range(len(sets))))
        rest = split(products(1) - moved)
        out_ref[...] = c_v[...] - dot3((w1h[...], w1l[...]), rest, NT)

    send_y0()
    send_x0()
    send_y1()
    send_x1()
    send_yt()
    turn_own()
    relay0()
    mul(0)
    relay1()
    gram_rows()
    mul(1)
    around(0)
    mul(2)
    around(1)
    mul(3)
    up(0)
    around(2)
    relay_t()
    up(1)
    around(3)
    pre0()
    up(2)
    swap_t()
    pre1()
    up(3)
    gram_over()
    last()
    copies.finish()


def on_device(vectors, householder, tfactors):
    v_t = jnp.swapaxes(householder, 1, 2)
    t_t = jnp.swapaxes(tfactors, 1, 2)
    anywhere = pl.BlockSpec(memory_space=pl.ANY)
    vmem = pltpu.VMEM
    tiles = lambda *shape: vmem((*shape, 8, 128), F32)
    scratch = [
        vmem((2, 8, 32, 512), F32),
        vmem((2, 8, 32, 256), F32),
        vmem((512, 128), F32),
        vmem((192, 512), BF16),
        vmem((192, 512), BF16),
        vmem((512, 256), BF16),
        vmem((512, 256), BF16),
        vmem((512, 256), BF16),
        vmem((512, 256), BF16),
        vmem((2, 128, 128), BF16),
        vmem((2, 128, 128), BF16),
        tiles(2, 2, NX, YL),
        pltpu.SemaphoreType.DMA((4,)),
        pltpu.SemaphoreType.DMA((N_COPIES,)),
        pltpu.SemaphoreType.DMA((N_COPIES,)),
    ]
    for pieces in SETS:
        n = 2 * len(pieces)
        with_gram = n + (GRAM in pieces)
        scratch += [
            tiles(2, YL, with_gram), tiles(YL, with_gram), tiles(YL, with_gram), tiles(7, with_gram),
            tiles(with_gram), tiles(NZ - 1, with_gram), tiles(2, YL, n),
        ]
    return pl.pallas_call(
        functools.partial(kernel, SETS, DIRECT),
        out_shape=pltpu.VMEM(vectors.shape, F32),
        in_specs=[anywhere] * 3,
        out_specs=pl.BlockSpec(memory_space=pltpu.VMEM),
        scratch_shapes=scratch,
        compiler_params=pltpu.CompilerParams(
            collective_id=0, has_side_effects=True, vmem_limit_bytes=60 * 2**20
        ),
        cost_estimate=pl.CostEstimate(flops=500_000_000, bytes_accessed=2_000_000, transcendentals=0),
        name="reflect",
    )(v_t, t_t, vectors)


def solution(mesh):
    return jax.shard_map(
        on_device,
        mesh=mesh,
        in_specs=(P("row", "col"), P(None, "row", "col"), P(None, None, "col")),
        out_specs=P("row", "col"),
        check_vma=False,
    )
```
